32 devices in a mesh: sector: 4 (over z), op: 8 (over y, x, core).
Axes of the slice: x: 2, y: 2, z: 4, core: 2. Of those that a mesh axis runs over, the one named last changes fastest.
Arguments:
- wavefunction: float32 [4, 512, 512], P('sector', 'op'), may hold values from -6 to 6
- diagonal: float32 [4, 512, 512], P('sector', 'op'), may hold values from 2 to 10
- left_blocks: bfloat16 [64, 512, 512], P('op'), may hold values from -1 to 1
- right_blocks: bfloat16 [64, 512, 512], P('op'), may hold values from -1 to 1
- coupling: int32 [4, 64], replicated, may hold values from 0 to 3
- sector_sizes: int32 [4], replicated, may hold values from 256 to 512
Outputs:
- vector: float32 [4, 512, 512], P('sector', 'op')
- energies: float32 [2], replicated
The draws below stay inside these ranges and needn't reach their ends.
All inputs are finite; a program needn't handle non-finite values.
Results may differ from the reference program's by a relative error of at most 0.0052.
Values may be sent and summed in bfloat16 or wider, within the bound.
A program may use at most 64 MiB of HBM per device.

```python
import math
import jax
import jax.numpy as jnp
import numpy as np
from jax import lax

BLOCK = 512
STEPS = 2
NSEC = 4
PAIRS = 64


def operator_draw(key):
    first, second = jax.random.split(key)
    spread = 1.0 / jnp.sqrt(jnp.float32(BLOCK))
    noise = jnp.clip(jax.random.normal(first, (PAIRS, BLOCK, BLOCK), jnp.float32), -4.0, 4.0)
    level = jax.random.uniform(second, (PAIRS, BLOCK), jnp.float32, 0.2, 0.3)
    ident = jnp.eye(BLOCK, dtype=jnp.float32)
    whole = noise * spread + ident[None, :, :] * level[:, :, None]
    return jnp.clip(whole, -1.0, 1.0).astype(jnp.bfloat16)


def draw_left_blocks(key, part):
    return operator_draw(jax.random.fold_in(key, 11))


def draw_right_blocks(key, part):
    return operator_draw(jax.random.fold_in(key, 23))


def set_ends(drawn, key, smallest, top_value):
    place = [jax.random.randint(jax.random.fold_in(key, axis), (), 0, length) for axis, length in enumerate(drawn.shape)]
    widest = drawn.shape.index(max(drawn.shape))
    neighbour = place[:widest] + [(place[widest] + 1) % drawn.shape[widest]] + place[widest + 1:]
    return drawn.at[tuple(place)].set(smallest).at[tuple(neighbour)].set(top_value)


def shard_levels(stream_key, extent, pieces, low, high):
    level, own = 1.0, jax.random.fold_in(stream_key, 6)
    for axis_at, shards_of in pieces:
        steps = jnp.exp(jax.random.uniform(jax.random.fold_in(own, axis_at), (shards_of,), jnp.float32, low / len(pieces), high / len(pieces)))
        level = level * jnp.repeat(steps, extent[axis_at] // shards_of).reshape([-1 if axis == axis_at else 1 for axis in range(len(extent))])
    return level


def rank_table(number_of, skew):
    portions = [(1 << 20) // math.isqrt(grade ** skew) + 1 for grade in range(1, number_of + 1)]
    scale = 1 + sum(portions) // (1 << 30)
    return np.cumsum(np.array([max(1, weight // scale) for weight in portions]))


def ranked(own_key, shape, number_of, skew):
    grid = rank_table(number_of, skew)
    lot = jax.random.randint(jax.random.fold_in(own_key, 1), shape, 0, int(grid[number_of - 1]))
    rank = jnp.searchsorted(jnp.asarray(grid, jnp.int32), lot, side="right")
    return jax.random.permutation(jax.random.fold_in(own_key, 2), number_of)[rank].astype(jnp.int32)


def scatter_about(stream_key, extent, scale, limit, cuts=(), kind=jnp.bfloat16):
    array = scale * jax.random.normal(stream_key, extent, jnp.float32)
    if cuts:
        array = array * shard_levels(stream_key, extent, cuts, -0.22, 0.18)
    return jnp.clip(array, -limit, limit).astype(kind)


def setup_inputs(seed: int = 0) -> dict:
    streams_of = jax.random.split(jax.random.key(seed), 7)
    wavefunction = scatter_about(streams_of[0], (NSEC, BLOCK, BLOCK), 1.0, 6.0, ((0, 4), (1, 8)), jnp.float32)
    diagonal = jnp.clip(2.0 + 8.0 * jax.random.uniform(streams_of[1], (NSEC, BLOCK, BLOCK), jnp.float32) ** shard_levels(streams_of[1], (NSEC, BLOCK, BLOCK), ((0, 4), (1, 8)), -0.2, 0.2), 2.0, 10.0)
    left_blocks = draw_left_blocks(jax.random.fold_in(streams_of[6], 71), 0)
    right_blocks = draw_right_blocks(jax.random.fold_in(streams_of[6], 71), 0)
    coupling = set_ends(ranked(streams_of[4], (NSEC, PAIRS), NSEC, 2), jax.random.fold_in(streams_of[4], 3), 0, NSEC - 1).astype(jnp.int32)
    sector_sizes = set_ends(jax.random.randint(streams_of[5], (NSEC,), BLOCK // 2, BLOCK + 1), jax.random.fold_in(streams_of[5], 1), BLOCK // 2, BLOCK).astype(jnp.int32)
    return {"wavefunction": wavefunction, "diagonal": diagonal, "left_blocks": left_blocks, "right_blocks": right_blocks, "coupling": coupling, "sector_sizes": sector_sizes}


def reference(wavefunction, diagonal, left_blocks, right_blocks, coupling, sector_sizes):
    positions = jnp.arange(BLOCK, dtype=jnp.int32)
    live = positions[None, :] < sector_sizes[:, None]
    mask = (live[:, :, None] & live[:, None, :]).astype(jnp.float32)
    current = wavefunction * mask
    left_wide = left_blocks.astype(jnp.float32)
    right_wide = right_blocks.astype(jnp.float32)
    collected = []
    for iteration in range(STEPS):
        current_low = current.astype(jnp.bfloat16)

        def sector_sigma(target):
            picked = jnp.take(current_low, coupling[target], axis=0).astype(jnp.float32)
            half = jnp.einsum('pij,pjk->pik', left_wide, picked).astype(jnp.bfloat16)
            return jnp.einsum('pik,plk->il', half.astype(jnp.float32), right_wide)
        sigma = lax.map(sector_sigma, jnp.arange(NSEC, dtype=jnp.int32)) * mask
        numerator = jnp.sum(current * sigma)
        denominator = jnp.sum(current * current)
        theta = numerator / (denominator + 1e-06)
        collected.append(theta)
        gap = diagonal - theta
        update = current - (sigma - theta * current) * gap / (gap * gap + 1.0)
        current = update * lax.rsqrt(jnp.mean(update * update) + 1e-06)
    return (current, jnp.stack(collected).astype(jnp.float32))
```

```python
import functools

import jax
import jax.numpy as jnp
from jax import lax
from jax.experimental import pallas as pl
from jax.experimental.pallas import tpu as pltpu
from jax.sharding import PartitionSpec as P

STEPS = 2
MESH = pl.DeviceIdType.MESH
F32 = jnp.float32
BF16 = jnp.bfloat16


def flip(value, mask):
    bit = 1
    while bit <= mask:
        if mask & bit:
            value = value + bit - 2 * bit * ((value // bit) % 2)
        bit *= 2
    return value


def folded(x):
    rows, width = x.shape
    x = jnp.sum(x.reshape(rows // 8, 8, width), axis=0)
    total = x[:, 0:128]
    for at in range(128, width, 128):
        total = total + x[:, at : at + 128]
    return total


def total_of(tile):
    return jnp.sum(jnp.sum(tile, axis=0, keepdims=True), axis=1, keepdims=True)


def kernel(
    sectors, ops, entry_total,
    coup, sizes, wf, diag, left, right,
    vec, energies,
    lv, rv, xa, xb, tt, acc, cur, s1_tx, s1_rx, s2_tx, s2_rx, sc_a, sc_b, sc_t,
    load_sem, x_send, x_recv, r1_send, r1_recv, r2_send, r2_recv, a_send, a_recv, b_send, b_recv,
):
    rows, width = wf.shape
    pairs = left.shape[0]
    chips = ops // 2
    half = chips // 2
    bits = chips.bit_length() - 1
    half_rows = half * 2 * rows
    z = lax.axis_index("sector")
    o = lax.axis_index("op")
    m, c = o // 2, o % 2
    top = m // half

    loads = [
        pltpu.make_async_copy(right, rv, load_sem.at[0]),
        pltpu.make_async_copy(left, lv, load_sem.at[1]),
    ]
    for load in loads:
        load.start()

    barrier = pltpu.get_barrier_semaphore()
    for k in range(1, ops):
        pl.semaphore_signal(barrier, inc=1, device_id=(z, flip(o, k)), device_id_type=MESH)
    for d in range(1, sectors):
        pl.semaphore_signal(barrier, inc=1, device_id=(flip(z, d), o), device_id_type=MESH)

    bound = sizes[z]
    row_ids = o * rows + lax.broadcasted_iota(jnp.int32, (rows, width), 0)
    col_ids = lax.broadcasted_iota(jnp.int32, (rows, width), 1)
    mask = ((row_ids < bound) & (col_ids < bound)).astype(F32)
    cur[...] = wf[...] * mask
    pl.semaphore_wait(barrier, ops - 1 + sectors - 1)

    def reduce_tile(red):
        sent = []
        for k in range(1, ops):
            copy = pltpu.make_async_remote_copy(
                sc_t.at[red], sc_a.at[red, o], a_send.at[red, k], a_recv.at[red, k],
                device_id=(z, flip(o, k)), device_id_type=MESH)
            copy.start()
            sent.append(copy)
        sc_a[red, o] = sc_t[red]

        def finish():
            for k in range(1, ops):
                pltpu.make_async_remote_copy(
                    sc_t.at[red], sc_a.at[red, flip(o, k)], a_send.at[red, k], a_recv.at[red, k],
                    device_id=(z, flip(o, k)), device_id_type=MESH).wait_recv()
            sc_b[red, z] = jnp.sum(sc_a[red], axis=0)
            for d in range(1, sectors):
                copy = pltpu.make_async_remote_copy(
                    sc_b.at[red, z], sc_b.at[red, z], b_send.at[red, d], b_recv.at[red, d],
                    device_id=(flip(z, d), o), device_id_type=MESH)
                copy.start()
                sent.append(copy)
            for d in range(1, sectors):
                pltpu.make_async_remote_copy(
                    sc_b.at[red, z], sc_b.at[red, flip(z, d)], b_send.at[red, d], b_recv.at[red, d],
                    device_id=(flip(z, d), o), device_id_type=MESH).wait_recv()
            both = jnp.sum(sc_b[red], axis=0)
            for copy in sent:
                copy.wait_send()
            return both

        return finish

    scale = None
    for step in range(STEPS):
        groups = (xa.at[step], xb.at[step])

        def place(d, g, core):
            chip = flip(m, g)
            row = pl.multiple_of((chip % half) * (2 * rows) + core * rows, rows)
            return flip(z, d), row, 2 * chip + core

        sent = []
        counter = [0]

        def send(d, g, core, to_z, to_m, to_core, to_d, to_g):
            sector, row, owner = place(d, g, core)
            source = groups[1 if g >= half else 0].at[sector, pl.ds(row, rows), :]
            target = groups[1 if to_g >= half else 0].at[sector, pl.ds(row, rows), :]
            copy = pltpu.make_async_remote_copy(
                source, target, x_send.at[step, counter[0]], x_recv.at[step, sector, owner],
                device_id=(to_z, 2 * to_m + to_core), device_id_type=MESH)
            counter[0] += 1
            copy.start()
            sent.append(copy)

        def arrive(d, g, core):
            sector, row, owner = place(d, g, core)
            slot = groups[1 if g >= half else 0].at[sector, pl.ds(row, rows), :]
            pltpu.make_async_remote_copy(
                slot, slot, x_send.at[step, 0], x_recv.at[step, sector, owner],
                device_id=(z, flip(o, 1)), device_id_type=MESH).wait_recv()

        own_sector, own_row, own_place = place(0, 0, c)
        groups[0][own_sector, pl.ds(own_row, rows), :] = cur[...].astype(BF16)

        def spread(d, g):
            if d == 0 and g == 0:
                for other in range(1, sectors):
                    send(0, 0, c, flip(z, other), m, c, other, 0)
            else:
                arrive(d, g, c)
            order = list(range(bits)) if d < sectors // 2 else list(range(bits))[::-1]
            last = -1
            for at, bit in enumerate(order):
                if g & (1 << bit):
                    last = at
            for bit in order[last + 1 :]:
                send(d, g, c, z, flip(m, 1 << bit), c, d, g ^ (1 << bit))
            send(d, g, c, z, m, 1 - c, d, g)

        plan = [(d, g) for d in range(sectors) for g in range(chips)]
        level = lambda g: bin(g).count("1")
        plan.sort(key=lambda dg: (dg[1] >= half and level(dg[1]) > 1, dg[0] + level(dg[1]), level(dg[1]), dg))
        early = [dg for dg in plan if not (dg[1] >= half and level(dg[1]) > 1)]
        late = [dg for dg in plan if dg not in early]

        def rotate(group, at):
            first = pl.multiple_of(at * half_rows, half_rows)
            for p in range(pairs):
                x = group[coup[z, o * pairs + p]]
                t = lax.dot_general(x, rv[p], (((1,), (1,)), ((), ())), preferred_element_type=F32)
                tt[p, pl.ds(first, half_rows), :] = t.astype(BF16)

        for d, g in early:
            spread(d, g)
        for d in range(sectors):
            for g in range(half):
                arrive(d, g, 1 - c)
        if step == 0:
            loads[0].wait()
        rotate(groups[0], top)
        for d, g in late:
            spread(d, g)
        for d in range(sectors):
            for g in range(half, chips):
                arrive(d, g, 1 - c)
        rotate(groups[1], 1 - top)
        if step == 0:
            loads[1].wait()

        pieces = []

        def r1(g):
            return pltpu.make_async_remote_copy(
                s1_tx.at[step, g], s1_rx.at[step, g], r1_send.at[step, g], r1_recv.at[step, g],
                device_id=(z, 2 * m + 1 - c), device_id_type=MESH)

        def r2(g):
            return pltpu.make_async_remote_copy(
                s2_tx.at[step, g], s2_rx.at[step, g], r2_send.at[step, g], r2_recv.at[step, g],
                device_id=(z, 2 * flip(m, g) + c), device_id_type=MESH)

        def block(which, g, core):
            row = pl.multiple_of((flip(m, g) % half) * (2 * rows) + core * rows, rows)
            return acc[which, pl.ds(row, rows), :]

        numer = None
        for which in (1, 0):
            at = top if which == 0 else 1 - top
            first = pl.multiple_of(at * half_rows, half_rows)
            total = None
            for p in range(pairs):
                part = jnp.dot(lv[p, pl.ds(first, half_rows), :], tt[p], preferred_element_type=F32)
                total = part if total is None else total + part
            acc[which] = total
            for g in reversed(range(which * half, which * half + half)):
                s1_tx[step, g] = block(which, g, 1 - c).astype(BF16)
                r1(g).start()
            tile = folded(groups[which][z].astype(F32) * acc[which])
            numer = tile if numer is None else numer + tile
        sc_t[step, 0] = numer
        sc_t[step, 1] = folded(cur[...] * cur[...])
        finish = reduce_tile(step)
        for g in reversed(range(1, chips)):
            r1(g).wait_recv()
            s2_tx[step, g] = (
                block(1 if g >= half else 0, g, c) + s1_rx[step, g].astype(F32)
            ).astype(BF16)
            r2(g).start()
        both = finish()
        r1(0).wait_recv()
        sigma = block(0, 0, c) + s1_rx[step, 0].astype(F32)
        for g in range(1, chips):
            r2(g).wait_recv()
            sigma = sigma + s2_rx[step, g].astype(F32)
        sigma = sigma * mask
        numer, denom = total_of(both[0]), total_of(both[1])
        if step == 0:
            theta = numer / (denom + 1e-06)
        else:
            scale = lax.rsqrt(denom / entry_total + 1e-06)
            theta = (scale * scale * numer) / (scale * scale * denom + 1e-06)
        energies[step] = theta[0, 0]
        gap = diag[...] - theta
        held = cur[...]
        update = held - (sigma - theta * held) * (gap / (gap * gap + 1.0))
        if step > 0:
            update = update * scale
        cur[...] = update
        for copy in sent:
            copy.wait_send()
        for g in range(chips):
            r1(g).wait_send()
        for g in range(1, chips):
            r2(g).wait_send()

    sc_t[STEPS, 0] = folded(cur[...] * cur[...])
    sc_t[STEPS, 1] = jnp.zeros((8, 128), F32)
    squares = total_of(reduce_tile(STEPS)()[0])
    vec[...] = cur[...] * lax.rsqrt(squares / entry_total + 1e-06)


def shards(sectors, ops, wavefunction, diagonal, left_blocks, right_blocks, coupling, sector_sizes):
    _, rows, width = wavefunction.shape
    pairs = left_blocks.shape[0]
    chips = ops // 2
    half_rows = ops * rows // 2
    entry_total = float(wavefunction.size * sectors * ops)
    vmem = pl.BlockSpec(memory_space=pltpu.VMEM)
    smem = pl.BlockSpec(memory_space=pltpu.SMEM)
    hbm = pl.BlockSpec(memory_space=pl.ANY)
    dma = pltpu.SemaphoreType.DMA
    sends = sectors * ops
    vector, energies = pl.pallas_call(
        functools.partial(kernel, sectors, ops, entry_total),
        out_shape=(
            jax.ShapeDtypeStruct((rows, width), F32),
            jax.ShapeDtypeStruct((STEPS,), F32),
        ),
        in_specs=[smem, smem, vmem, vmem, hbm, hbm],
        out_specs=(vmem, smem),
        scratch_shapes=[
            pltpu.VMEM(left_blocks.shape, BF16),
            pltpu.VMEM(right_blocks.shape, BF16),
            pltpu.VMEM((STEPS, sectors, half_rows, width), BF16),
            pltpu.VMEM((STEPS, sectors, half_rows, width), BF16),
            pltpu.VMEM((pairs, 2 * half_rows, width), BF16),
            pltpu.VMEM((2, half_rows, width), F32),
            pltpu.VMEM((rows, width), F32),
            pltpu.VMEM((STEPS, chips, rows, width), BF16),
            pltpu.VMEM((STEPS, chips, rows, width), BF16),
            pltpu.VMEM((STEPS, chips, rows, width), BF16),
            pltpu.VMEM((STEPS, chips, rows, width), BF16),
            pltpu.VMEM((STEPS + 1, ops, 2, 8, 128), F32),
            pltpu.VMEM((STEPS + 1, sectors, 2, 8, 128), F32),
            pltpu.VMEM((STEPS + 1, 2, 8, 128), F32),
            dma((2,)),
            dma((STEPS, sends)),
            dma((STEPS, sectors, ops)),
            dma((STEPS, chips)),
            dma((STEPS, chips)),
            dma((STEPS, chips)),
            dma((STEPS, chips)),
            dma((STEPS + 1, ops)),
            dma((STEPS + 1, ops)),
            dma((STEPS + 1, sectors)),
            dma((STEPS + 1, sectors)),
        ],
        compiler_params=pltpu.CompilerParams(
            collective_id=0, has_side_effects=True, vmem_limit_bytes=48 * 1024 * 1024
        ),
    )(coupling, sector_sizes, wavefunction[0], diagonal[0], left_blocks, right_blocks)
    return vector[None], energies


def solution(mesh):
    in_specs = (
        P("sector", "op", None),
        P("sector", "op", None),
        P("op", None, None),
        P("op", None, None),
        P(),
        P(),
    )
    out_specs = (P("sector", "op", None), P())
    body = functools.partial(shards, mesh.shape["sector"], mesh.shape["op"])
    return jax.shard_map(body, mesh=mesh, in_specs=in_specs, out_specs=out_specs, check_vma=False)
```

```python
import functools

import jax
import jax.numpy as jnp
from jax import lax
from jax.experimental import pallas as pl
from jax.experimental.pallas import tpu as pltpu
from jax.sharding import PartitionSpec as P

STEPS = 2
MESH = pl.DeviceIdType.MESH
F32 = jnp.float32
BF16 = jnp.bfloat16


def flip(value, mask):
    bit = 1
    while bit <= mask:
        if mask & bit:
            value = value + bit - 2 * bit * ((value // bit) % 2)
        bit *= 2
    return value


def folded(x):
    rows, width = x.shape
    x = jnp.sum(x.reshape(rows // 8, 8, width), axis=0)
    total = x[:, 0:128]
    for at in range(128, width, 128):
        total = total + x[:, at : at + 128]
    return total


def total_of(tile):
    return jnp.sum(jnp.sum(tile, axis=0, keepdims=True), axis=1, keepdims=True)


def kernel(
    sectors, ops, entry_total,
    coup_in, sizes_in, wf_in, diag_in, left, right,
    vec, energies,
    coup, sizes, wf, diag, lv, rv, xa, xb, tt, acc, cur, s1_tx, s1_rx, s2_tx, s2_rx, sc_a, sc_b, sc_t,
    load_sem, x_send, x_recv, r1_send, r1_recv, r2_send, r2_recv, a_send, a_recv, b_send, b_recv,
):
    rows, width = wf.shape
    pairs = left.shape[0]
    chips = ops // 2
    half = chips // 2
    bits = chips.bit_length() - 1
    half_rows = half * 2 * rows
    z = lax.axis_index("sector")
    o = lax.axis_index("op")
    m, c = o // 2, o % 2
    top = m // half

    small = [(wf_in, wf), (sizes_in, sizes), (coup_in, coup), (diag_in, diag)]
    small = [
        pltpu.make_async_copy(src, dst, load_sem.at[at]) for at, (src, dst) in enumerate(small)
    ]
    loads = [pltpu.make_async_copy(right, rv, load_sem.at[4])] + [
        pltpu.make_async_copy(left.at[p], lv.at[:, pl.ds(p * width, width)], load_sem.at[5 + p])
        for p in range(pairs)
    ]
    for load in small:
        load.start()

    barrier = pltpu.get_barrier_semaphore()
    for k in range(1, ops):
        pl.semaphore_signal(barrier, inc=1, device_id=(z, flip(o, k)), device_id_type=MESH)
    for d in range(1, sectors):
        pl.semaphore_signal(barrier, inc=1, device_id=(flip(z, d), o), device_id_type=MESH)

    for load in loads:
        load.start()
    small[0].wait()
    small[1].wait()
    bound = sizes[z]
    row_ids = o * rows + lax.broadcasted_iota(jnp.int32, (rows, width), 0)
    col_ids = lax.broadcasted_iota(jnp.int32, (rows, width), 1)
    mask = ((row_ids < bound) & (col_ids < bound)).astype(F32)
    cur[...] = wf[...] * mask
    pl.semaphore_wait(barrier, ops - 1 + sectors - 1)

    def reduce_tile(red):
        sent = []
        for k in range(1, ops):
            copy = pltpu.make_async_remote_copy(
                sc_t.at[red], sc_a.at[red, o], a_send.at[red, k], a_recv.at[red, k],
                device_id=(z, flip(o, k)), device_id_type=MESH)
            copy.start()
            sent.append(copy)
        sc_a[red, o] = sc_t[red]

        def finish():
            for k in range(1, ops):
                pltpu.make_async_remote_copy(
                    sc_t.at[red], sc_a.at[red, flip(o, k)], a_send.at[red, k], a_recv.at[red, k],
                    device_id=(z, flip(o, k)), device_id_type=MESH).wait_recv()
            sc_b[red, z] = jnp.sum(sc_a[red], axis=0)
            for d in range(1, sectors):
                copy = pltpu.make_async_remote_copy(
                    sc_b.at[red, z], sc_b.at[red, z], b_send.at[red, d], b_recv.at[red, d],
                    device_id=(flip(z, d), o), device_id_type=MESH)
                copy.start()
                sent.append(copy)
            for d in range(1, sectors):
                pltpu.make_async_remote_copy(
                    sc_b.at[red, z], sc_b.at[red, flip(z, d)], b_send.at[red, d], b_recv.at[red, d],
                    device_id=(flip(z, d), o), device_id_type=MESH).wait_recv()
            both = jnp.sum(sc_b[red], axis=0)
            for copy in sent:
                copy.wait_send()
            return both

        return finish

    scale = None
    for step in range(STEPS):
        groups = (xa.at[step], xb.at[step])

        def place(r, g, core):
            chip = flip(m, g)
            row = pl.multiple_of((chip % half) * (2 * rows) + core * rows, rows)
            return z + r, row, 2 * chip + core

        sent = []

        def inside(r):
            return jnp.logical_and(z + r >= 0, z + r < sectors)

        def send(pred, r, g, to_z, to_m, to_core, to_g):
            at = len(sent)

            def copy():
                sector, row, owner = place(r, g, c)
                source = groups[1 if g >= half else 0].at[sector, pl.ds(row, rows), :]
                target = groups[1 if to_g >= half else 0].at[sector, pl.ds(row, rows), :]
                return pltpu.make_async_remote_copy(
                    source, target, x_send.at[at], x_recv.at[step, sector, owner],
                    device_id=(to_z, 2 * to_m + to_core), device_id_type=MESH)

            sent.append((pred, copy))
            pl.when(pred)(lambda: copy().start())

        def arrive(r, g, core):
            sector, row, owner = place(r, g, core)
            slot = groups[1 if g >= half else 0].at[sector, pl.ds(row, rows), :]
            pltpu.make_async_remote_copy(
                slot, slot, x_send.at[0], x_recv.at[step, sector, owner],
                device_id=(z, flip(o, 1)), device_id_type=MESH).wait_recv()

        own_sector, own_row, _ = place(0, 0, c)
        groups[0][own_sector, pl.ds(own_row, rows), :] = cur[...].astype(BF16)

        def spread(r, g):
            here = inside(r)
            if r or g:
                pl.when(here)(lambda: arrive(r, g, c))
            if g == 0 and r <= 0:
                send(jnp.logical_and(here, z + 1 < sectors), r, 0, z + 1, m, c, 0)
            if g == 0 and r >= 0:
                send(jnp.logical_and(here, z >= 1), r, 0, z - 1, m, c, 0)
            order = list(range(bits)) if r % 2 == 0 else list(range(bits))[::-1]
            last = -1
            for at, bit in enumerate(order):
                if g & (1 << bit):
                    last = at
            for bit in order[last + 1 :]:
                send(here, r, g, z, flip(m, 1 << bit), c, g ^ (1 << bit))
            send(here, r, g, z, m, 1 - c, g)

        def arrive_sibling(first, end):
            for r in range(1 - sectors, sectors):

                @pl.when(inside(r))
                def _():
                    for g in range(first, end):
                        arrive(r, g, 1 - c)

        level = lambda g: bin(g).count("1")
        is_late = lambda rg: rg[1] >= half and level(rg[1]) > 1
        plan = [(r, g) for r in range(1 - sectors, sectors) for g in range(chips)]
        plan.sort(key=lambda rg: (is_late(rg), abs(rg[0]) + level(rg[1]), level(rg[1]), abs(rg[0]), rg))
        early = [rg for rg in plan if not is_late(rg)]
        late = [rg for rg in plan if is_late(rg)]

        def rotate(group, at):
            first = pl.multiple_of(at * half_rows, half_rows)
            for p in range(pairs):
                x = group[coup[z, o * pairs + p]]
                t = lax.dot_general(x, rv[p], (((1,), (1,)), ((), ())), preferred_element_type=F32)
                tt[pl.ds(pl.multiple_of(p * width + first, half_rows), half_rows), :] = t.astype(BF16)

        for r, g in early:
            spread(r, g)
        arrive_sibling(0, half)
        if step == 0:
            small[2].wait()
            loads[0].wait()
        rotate(groups[0], top)
        for r, g in late:
            spread(r, g)
        arrive_sibling(half, chips)
        rotate(groups[1], 1 - top)
        if step == 0:
            for load in loads[1:] + small[3:]:
                load.wait()

        def r1(g):
            return pltpu.make_async_remote_copy(
                s1_tx.at[step, g], s1_rx.at[step, g], r1_send.at[step, g], r1_recv.at[step, g],
                device_id=(z, 2 * m + 1 - c), device_id_type=MESH)

        def r2(g):
            return pltpu.make_async_remote_copy(
                s2_tx.at[step, g], s2_rx.at[step, g], r2_send.at[step, g], r2_recv.at[step, g],
                device_id=(z, 2 * flip(m, g) + c), device_id_type=MESH)

        def block(which, g, core):
            row = pl.multiple_of((flip(m, g) % half) * (2 * rows) + core * rows, rows)
            return acc[which, pl.ds(row, rows), :]

        def partial(which, column, end):
            at = top if which == 0 else 1 - top
            first = pl.multiple_of(at * half_rows, half_rows)
            acc[which, :, column:end] = jnp.dot(
                lv[pl.ds(first, half_rows), :], tt[:, column:end], preferred_element_type=F32)

        def to_sibling(which):
            for g in reversed(range(which * half, which * half + half)):
                s1_tx[step, g] = block(which, g, 1 - c).astype(BF16)
                r1(g).start()

        def to_chips(which):
            for g in reversed(range(max(1, which * half), which * half + half)):
                r1(g).wait_recv()
                s2_tx[step, g] = (block(which, g, c) + s1_rx[step, g].astype(F32)).astype(BF16)
                r2(g).start()

        partial(1, 0, width)
        to_sibling(1)
        partial(0, 0, width // 2)
        to_chips(1)
        partial(0, width // 2, width)
        to_sibling(0)
        sc_t[step, 0] = folded(xa[step, z].astype(F32) * acc[0]) + folded(xb[step, z].astype(F32) * acc[1])
        sc_t[step, 1] = folded(cur[...] * cur[...])
        finish = reduce_tile(step)
        to_chips(0)
        both = finish()
        r1(0).wait_recv()
        sigma = block(0, 0, c) + s1_rx[step, 0].astype(F32)
        for g in range(1, chips):
            r2(g).wait_recv()
            sigma = sigma + s2_rx[step, g].astype(F32)
        sigma = sigma * mask
        numer, denom = total_of(both[0]), total_of(both[1])
        if step == 0:
            theta = numer / (denom + 1e-06)
        else:
            scale = lax.rsqrt(denom / entry_total + 1e-06)
            theta = (scale * scale * numer) / (scale * scale * denom + 1e-06)
        energies[step] = theta[0, 0]
        gap = diag[...] - theta
        held = cur[...]
        update = held - (sigma - theta * held) * (gap / (gap * gap + 1.0))
        if step > 0:
            update = update * scale
        cur[...] = update
        for pred, copy in sent:
            pl.when(pred)(lambda copy=copy: copy().wait_send())
        for g in range(chips):
            r1(g).wait_send()
        for g in range(1, chips):
            r2(g).wait_send()

    sc_t[STEPS, 0] = folded(cur[...] * cur[...])
    sc_t[STEPS, 1] = jnp.zeros((8, 128), F32)
    squares = total_of(reduce_tile(STEPS)()[0])
    vec[...] = cur[...] * lax.rsqrt(squares / entry_total + 1e-06)


def shards(sectors, ops, wavefunction, diagonal, left_blocks, right_blocks, coupling, sector_sizes):
    _, rows, width = wavefunction.shape
    pairs = left_blocks.shape[0]
    chips = ops // 2
    half_rows = ops * rows // 2
    entry_total = float(wavefunction.size * sectors * ops)
    vmem = pl.BlockSpec(memory_space=pltpu.VMEM)
    smem = pl.BlockSpec(memory_space=pltpu.SMEM)
    hbm = pl.BlockSpec(memory_space=pl.ANY)
    dma = pltpu.SemaphoreType.DMA
    sends = (2 * sectors - 1) * 2 * chips + 2
    vector, energies = pl.pallas_call(
        functools.partial(kernel, sectors, ops, entry_total),
        out_shape=(
            jax.ShapeDtypeStruct((rows, width), F32),
            jax.ShapeDtypeStruct((STEPS,), F32),
        ),
        in_specs=[hbm] * 6,
        out_specs=(vmem, smem),
        scratch_shapes=[
            pltpu.SMEM(coupling.shape, jnp.int32),
            pltpu.SMEM(sector_sizes.shape, jnp.int32),
            pltpu.VMEM((rows, width), F32),
            pltpu.VMEM((rows, width), F32),
            pltpu.VMEM((width, pairs * width), BF16),
            pltpu.VMEM(right_blocks.shape, BF16),
            pltpu.VMEM((STEPS, sectors, half_rows, width), BF16),
            pltpu.VMEM((STEPS, sectors, half_rows, width), BF16),
            pltpu.VMEM((pairs * width, width), BF16),
            pltpu.VMEM((2, half_rows, width), F32),
            pltpu.VMEM((rows, width), F32),
            pltpu.VMEM((STEPS, chips, rows, width), BF16),
            pltpu.VMEM((STEPS, chips, rows, width), BF16),
            pltpu.VMEM((STEPS, chips, rows, width), BF16),
            pltpu.VMEM((STEPS, chips, rows, width), BF16),
            pltpu.VMEM((STEPS + 1, ops, 2, 8, 128), F32),
            pltpu.VMEM((STEPS + 1, sectors, 2, 8, 128), F32),
            pltpu.VMEM((STEPS + 1, 2, 8, 128), F32),
            dma((5 + pairs,)),
            dma((sends,)),
            dma((STEPS, sectors, ops)),
            dma((STEPS, chips)),
            dma((STEPS, chips)),
            dma((STEPS, chips)),
            dma((STEPS, chips)),
            dma((STEPS + 1, ops)),
            dma((STEPS + 1, ops)),
            dma((STEPS + 1, sectors)),
            dma((STEPS + 1, sectors)),
        ],
        compiler_params=pltpu.CompilerParams(
            collective_id=0, has_side_effects=True, vmem_limit_bytes=62 * 1024 * 1024
        ),
    )(coupling, sector_sizes, wavefunction[0], diagonal[0], left_blocks, right_blocks)
    return vector[None], energies


def solution(mesh):
    in_specs = (
        P("sector", "op", None),
        P("sector", "op", None),
        P("op", None, None),
        P("op", None, None),
        P(),
        P(),
    )
    out_specs = (P("sector", "op", None), P())
    body = functools.partial(shards, mesh.shape["sector"], mesh.shape["op"])
    return jax.shard_map(body, mesh=mesh, in_specs=in_specs, out_specs=out_specs, check_vma=False)
```

```python
import functools

import jax
import jax.numpy as jnp
from jax import lax
from jax.experimental import pallas as pl
from jax.experimental.pallas import tpu as pltpu
from jax.sharding import PartitionSpec as P

STEPS = 2
MESH = pl.DeviceIdType.MESH
F32 = jnp.float32
BF16 = jnp.bfloat16


def flip(value, mask):
    bit = 1
    while bit <= mask:
        if mask & bit:
            value = value + bit - 2 * bit * ((value // bit) % 2)
        bit *= 2
    return value


def folded(x):
    rows, width = x.shape
    x = jnp.sum(x.reshape(rows // 8, 8, width), axis=0)
    total = x[:, 0:128]
    for at in range(128, width, 128):
        total = total + x[:, at : at + 128]
    return total


def total_of(tile):
    return jnp.sum(jnp.sum(tile, axis=0, keepdims=True), axis=1, keepdims=True)


def kernel(
    sectors, ops, entry_total,
    coup_in, sizes_in, wf_in, diag_in, left, right,
    vec, energies,
    coup, sizes, wf, diag, lv, rv, xa, xb, tt, acc, cur, s1_tx, s1_rx, s2_tx, s2_rx, sc_a, sc_b, sc_t,
    load_sem, x_send, x_recv, r1_send, r1_recv, r2_send, r2_recv, a_send, a_recv, b_send, b_recv,
):
    rows, width = wf.shape
    pairs = left.shape[0]
    chips = ops // 2
    half = chips // 2
    bits = chips.bit_length() - 1
    half_rows = half * 2 * rows
    z = lax.axis_index("sector")
    o = lax.axis_index("op")
    m, c = o // 2, o % 2
    top = m // half
    chip_at = [flip(m, g) for g in range(chips)]
    op_at = [flip(o, k) for k in range(ops)]
    z_at = [flip(z, d) for d in range(sectors)]
    row_at = [
        [pl.multiple_of((chip_at[g] % half) * (2 * rows) + core * rows, rows) for core in (c, 1 - c)]
        for g in range(chips)
    ]
    first_at = [pl.multiple_of(at * half_rows, half_rows) for at in (top, 1 - top)]

    small = [(wf_in, wf), (sizes_in, sizes), (coup_in, coup), (diag_in, diag)]
    small = [
        pltpu.make_async_copy(src, dst, load_sem.at[at]) for at, (src, dst) in enumerate(small)
    ]
    loads = [pltpu.make_async_copy(right, rv, load_sem.at[4])] + [
        pltpu.make_async_copy(left.at[p], lv.at[:, pl.ds(p * width, width)], load_sem.at[5 + p])
        for p in range(pairs)
    ]
    for load in small:
        load.start()

    barrier = pltpu.get_barrier_semaphore()
    for k in range(1, ops):
        pl.semaphore_signal(barrier, inc=1, device_id=(z, op_at[k]), device_id_type=MESH)
    for d in range(1, sectors):
        pl.semaphore_signal(barrier, inc=1, device_id=(z_at[d], o), device_id_type=MESH)

    for load in loads:
        load.start()
    small[0].wait()
    small[1].wait()
    bound = sizes[z]
    row_ids = o * rows + lax.broadcasted_iota(jnp.int32, (rows, width), 0)
    col_ids = lax.broadcasted_iota(jnp.int32, (rows, width), 1)
    mask = ((row_ids < bound) & (col_ids < bound)).astype(F32)
    cur[...] = wf[...] * mask
    pl.semaphore_wait(barrier, ops - 1 + sectors - 1)

    def reduce_tile(red):
        sent = []
        for k in range(1, ops):
            copy = pltpu.make_async_remote_copy(
                sc_t.at[red], sc_a.at[red, o], a_send.at[red, k], a_recv.at[red, k],
                device_id=(z, op_at[k]), device_id_type=MESH)
            copy.start()
            sent.append(copy)
        sc_a[red, o] = sc_t[red]

        def finish():
            for k in range(1, ops):
                pltpu.make_async_remote_copy(
                    sc_t.at[red], sc_a.at[red, op_at[k]], a_send.at[red, k], a_recv.at[red, k],
                    device_id=(z, op_at[k]), device_id_type=MESH).wait_recv()
            sc_b[red, z] = jnp.sum(sc_a[red], axis=0)
            for d in range(1, sectors):
                copy = pltpu.make_async_remote_copy(
                    sc_b.at[red, z], sc_b.at[red, z], b_send.at[red, d], b_recv.at[red, d],
                    device_id=(z_at[d], o), device_id_type=MESH)
                copy.start()
                sent.append(copy)
            for d in range(1, sectors):
                pltpu.make_async_remote_copy(
                    sc_b.at[red, z], sc_b.at[red, z_at[d]], b_send.at[red, d], b_recv.at[red, d],
                    device_id=(z_at[d], o), device_id_type=MESH).wait_recv()
            both = jnp.sum(sc_b[red], axis=0)
            for copy in sent:
                copy.wait_send()
            return both

        return finish

    scale = None
    for step in range(STEPS):
        groups = (xa.at[step], xb.at[step])

        sent = []

        def slot(d, g, other):
            first = (2 * (g % half) + other) * rows
            return groups[1 if g >= half else 0].at[d, pl.ds(first, rows), :]

        def send(d, g, to, to_d, to_g, other):
            copy = pltpu.make_async_remote_copy(
                slot(d, g, 0), slot(to_d, to_g, other),
                x_send.at[step, len(sent)], x_recv.at[step, to_d, to_g, other],
                device_id=to, device_id_type=MESH)
            copy.start()
            sent.append(copy)

        def arrive(d, g, other):
            here = slot(d, g, other)
            pltpu.make_async_remote_copy(
                here, here, x_send.at[step, 0], x_recv.at[step, d, g, other],
                device_id=(z, op_at[1]), device_id_type=MESH).wait_recv()

        groups[0][0, 0:rows, :] = cur[...].astype(BF16)

        def spread(d, g):
            if d or g:
                arrive(d, g, 0)
            order = list(range(bits)) if d % 2 == 0 else list(range(bits))[::-1]
            last = -1
            for at, bit in enumerate(order):
                if g & (1 << bit):
                    last = at
            if d == 0 and g == 0 and sectors > 1:
                send(0, 0, (z_at[1], o), 1, 0, 0)
            for bit in order[last + 1 :]:
                send(d, g, (z, op_at[2 << bit]), d, g ^ (1 << bit), 0)
            if d == 0 and g == 0:
                for far in range(2, sectors):
                    send(0, 0, (z_at[far], o), far, 0, 0)
            send(d, g, (z, op_at[1]), d, g, 1)

        level = lambda g: bin(g).count("1")
        is_late = lambda dg: dg[1] >= half and level(dg[1]) > 1
        plan = [(d, g) for d in range(sectors) for g in range(chips)]
        plan.sort(key=lambda dg: (is_late(dg), dg[0] + level(dg[1]), dg))
        early = [dg for dg in plan if not is_late(dg)]
        late = [dg for dg in plan if is_late(dg)]

        def rotate(which):
            for p in range(pairs):
                x = groups[which][coup[z, o * pairs + p] ^ z]
                t = lax.dot_general(x, rv[p], (((1,), (1,)), ((), ())), preferred_element_type=F32)
                t = t.astype(BF16)
                for g in range(half):
                    for other in range(2):
                        row = pl.multiple_of(p * width + first_at[which] + row_at[g + which * half][other], rows)
                        first = (2 * g + other) * rows
                        tt[pl.ds(row, rows), :] = t[first : first + rows]

        def arrive_sibling(first, end):
            for d in range(sectors):
                for g in range(first, end):
                    arrive(d, g, 1)

        for d, g in early:
            spread(d, g)
        arrive_sibling(0, half)
        if step == 0:
            small[2].wait()
            loads[0].wait()
        rotate(0)
        for d, g in late:
            spread(d, g)
        arrive_sibling(half, chips)
        rotate(1)
        if step == 0:
            for load in loads[1:] + small[3:]:
                load.wait()

        def r1(g):
            return pltpu.make_async_remote_copy(
                s1_tx.at[step, g], s1_rx.at[step, g], r1_send.at[step, g], r1_recv.at[step, g],
                device_id=(z, op_at[1]), device_id_type=MESH)

        def r2(g):
            return pltpu.make_async_remote_copy(
                s2_tx.at[step, g], s2_rx.at[step, g], r2_send.at[step, g], r2_recv.at[step, g],
                device_id=(z, op_at[2 * g]), device_id_type=MESH)

        def block(g, other):
            return acc[1 if g >= half else 0, pl.ds(row_at[g][other], rows), :]

        def inner(g, other):
            return folded(slot(0, g, other)[...].astype(F32) * block(g, other))

        def partial(which, column, end):
            acc[which, :, column:end] = jnp.dot(
                lv[pl.ds(first_at[which], half_rows), :], tt[:, column:end], preferred_element_type=F32)

        def to_sibling(which):
            for g in reversed(range(which * half, which * half + half)):
                s1_tx[step, g] = block(g, 1).astype(BF16)
                r1(g).start()

        def to_chips(which):
            for g in reversed(range(max(1, which * half), which * half + half)):
                r1(g).wait_recv()
                s2_tx[step, g] = (block(g, 0) + s1_rx[step, g].astype(F32)).astype(BF16)
                r2(g).start()

        partial(1, 0, width)
        to_sibling(1)
        partial(0, 0, width // 2)
        to_chips(1)
        partial(0, width // 2, width)
        to_sibling(0)
        sc_t[step, 0] = sum(inner(g, other) for g in range(chips) for other in range(2))
        sc_t[step, 1] = folded(cur[...] * cur[...])
        finish = reduce_tile(step)
        to_chips(0)
        both = finish()
        r1(0).wait_recv()
        sigma = block(0, 0) + s1_rx[step, 0].astype(F32)
        for g in range(1, chips):
            r2(g).wait_recv()
            sigma = sigma + s2_rx[step, g].astype(F32)
        sigma = sigma * mask
        numer, denom = total_of(both[0]), total_of(both[1])
        if step == 0:
            theta = numer / (denom + 1e-06)
        else:
            scale = lax.rsqrt(denom / entry_total + 1e-06)
            theta = (scale * scale * numer) / (scale * scale * denom + 1e-06)
        energies[step] = theta[0, 0]
        gap = diag[...] - theta
        held = cur[...]
        update = held - (sigma - theta * held) * (gap / (gap * gap + 1.0))
        if step > 0:
            update = update * scale
        cur[...] = update
        for copy in sent:
            copy.wait_send()
        for g in range(chips):
            r1(g).wait_send()
        for g in range(1, chips):
            r2(g).wait_send()

    sc_t[STEPS, 0] = folded(cur[...] * cur[...])
    sc_t[STEPS, 1] = jnp.zeros((8, 128), F32)
    squares = total_of(reduce_tile(STEPS)()[0])
    vec[...] = cur[...] * lax.rsqrt(squares / entry_total + 1e-06)


def shards(sectors, ops, wavefunction, diagonal, left_blocks, right_blocks, coupling, sector_sizes):
    _, rows, width = wavefunction.shape
    pairs = left_blocks.shape[0]
    chips = ops // 2
    half_rows = ops * rows // 2
    entry_total = float(wavefunction.size * sectors * ops)
    vmem = pl.BlockSpec(memory_space=pltpu.VMEM)
    smem = pl.BlockSpec(memory_space=pltpu.SMEM)
    hbm = pl.BlockSpec(memory_space=pl.ANY)
    dma = pltpu.SemaphoreType.DMA
    vector, energies = pl.pallas_call(
        functools.partial(kernel, sectors, ops, entry_total),
        out_shape=(
            jax.ShapeDtypeStruct((rows, width), F32),
            jax.ShapeDtypeStruct((STEPS,), F32),
        ),
        in_specs=[hbm] * 6,
        out_specs=(vmem, smem),
        scratch_shapes=[
            pltpu.SMEM(coupling.shape, jnp.int32),
            pltpu.SMEM(sector_sizes.shape, jnp.int32),
            pltpu.VMEM((rows, width), F32),
            pltpu.VMEM((rows, width), F32),
            pltpu.VMEM((width, pairs * width), BF16),
            pltpu.VMEM(right_blocks.shape, BF16),
            pltpu.VMEM((STEPS, sectors, half_rows, width), BF16),
            pltpu.VMEM((STEPS, sectors, half_rows, width), BF16),
            pltpu.VMEM((pairs * width, width), BF16),
            pltpu.VMEM((2, half_rows, width), F32),
            pltpu.VMEM((rows, width), F32),
            pltpu.VMEM((STEPS, chips, rows, width), BF16),
            pltpu.VMEM((STEPS, chips, rows, width), BF16),
            pltpu.VMEM((STEPS, chips, rows, width), BF16),
            pltpu.VMEM((STEPS, chips, rows, width), BF16),
            pltpu.VMEM((STEPS + 1, ops, 2, 8, 128), F32),
            pltpu.VMEM((STEPS + 1, sectors, 2, 8, 128), F32),
            pltpu.VMEM((STEPS + 1, 2, 8, 128), F32),
            dma((5 + pairs,)),
            dma((STEPS, sectors * ops)),
            dma((STEPS, sectors, chips, 2)),
            dma((STEPS, chips)),
            dma((STEPS, chips)),
            dma((STEPS, chips)),
            dma((STEPS, chips)),
            dma((STEPS + 1, ops)),
            dma((STEPS + 1, ops)),
            dma((STEPS + 1, sectors)),
            dma((STEPS + 1, sectors)),
        ],
        compiler_params=pltpu.CompilerParams(
            collective_id=0, has_side_effects=True, vmem_limit_bytes=62 * 1024 * 1024
        ),
    )(coupling, sector_sizes, wavefunction[0], diagonal[0], left_blocks, right_blocks)
    return vector[None], energies


def solution(mesh):
    in_specs = (
        P("sector", "op", None),
        P("sector", "op", None),
        P("op", None, None),
        P("op", None, None),
        P(),
        P(),
    )
    out_specs = (P("sector", "op", None), P())
    body = functools.partial(shards, mesh.shape["sector"], mesh.shape["op"])
    return jax.shard_map(body, mesh=mesh, in_specs=in_specs, out_specs=out_specs, check_vma=False)
```

```python
import functools

import jax
import jax.numpy as jnp
from jax import lax
from jax.experimental import pallas as pl
from jax.experimental.pallas import tpu as pltpu
from jax.sharding import PartitionSpec as P

STEPS = 2
MESH = pl.DeviceIdType.MESH
F32 = jnp.float32
BF16 = jnp.bfloat16


def flip(value, mask):
    bit = 1
    while bit <= mask:
        if mask & bit:
            value = value + bit - 2 * bit * ((value // bit) % 2)
        bit *= 2
    return value


def folded(x):
    rows, width = x.shape
    x = jnp.sum(x.reshape(rows // 8, 8, width), axis=0)
    total = x[:, 0:128]
    for at in range(128, width, 128):
        total = total + x[:, at : at + 128]
    return total


def total_of(tile):
    return jnp.sum(jnp.sum(tile, axis=0, keepdims=True), axis=1, keepdims=True)


def kernel(
    sectors, ops, entry_total,
    coup_in, sizes_in, wf_in, diag_in, left, right,
    vec, energies,
    coup, sizes, wf, diag, lv, rv, xa, xb, tt, acc, cur, s1_tx, s1_rx, s2_tx, s2_rx, sc_a, sc_b, sc_t,
    load_sem, x_send, x_recv, r1_send, r1_recv, r2_send, r2_recv, a_send, a_recv, b_send, b_recv,
):
    rows, width = wf.shape
    pairs = left.shape[0]
    chips = ops // 2
    half = chips // 2
    bits = chips.bit_length() - 1
    half_rows = half * 2 * rows
    z = lax.axis_index("sector")
    o = lax.axis_index("op")
    m, c = o // 2, o % 2
    top = m // half
    chip_at = [flip(m, g) for g in range(chips)]
    op_at = [flip(o, k) for k in range(ops)]
    z_at = [flip(z, d) for d in range(sectors)]
    row_at = [
        [pl.multiple_of((chip_at[g] % half) * (2 * rows) + core * rows, rows) for core in (c, 1 - c)]
        for g in range(chips)
    ]
    first_at = [pl.multiple_of(at * half_rows, half_rows) for at in (top, 1 - top)]

    small = [(wf_in, wf), (sizes_in, sizes), (coup_in, coup), (diag_in, diag)]
    small = [
        pltpu.make_async_copy(src, dst, load_sem.at[at]) for at, (src, dst) in enumerate(small)
    ]
    loads = [
        pltpu.make_async_copy(right, rv, load_sem.at[4]),
        pltpu.make_async_copy(left, lv, load_sem.at[5]),
    ]
    for load in small:
        load.start()

    barrier = pltpu.get_barrier_semaphore()
    for k in range(1, ops):
        pl.semaphore_signal(barrier, inc=1, device_id=(z, op_at[k]), device_id_type=MESH)
    for d in range(1, sectors):
        pl.semaphore_signal(barrier, inc=1, device_id=(z_at[d], o), device_id_type=MESH)

    for load in loads:
        load.start()
    small[0].wait()
    small[1].wait()
    bound = sizes[z]
    row_ids = o * rows + lax.broadcasted_iota(jnp.int32, (rows, width), 0)
    col_ids = lax.broadcasted_iota(jnp.int32, (rows, width), 1)
    mask = ((row_ids < bound) & (col_ids < bound)).astype(F32)
    cur[...] = wf[...] * mask
    pl.semaphore_wait(barrier, ops - 1 + sectors - 1)

    def reduce_tile(red):
        sent = []
        for k in range(1, ops):
            copy = pltpu.make_async_remote_copy(
                sc_t.at[red], sc_a.at[red, o], a_send.at[red, k], a_recv.at[red, k],
                device_id=(z, op_at[k]), device_id_type=MESH)
            copy.start()
            sent.append(copy)
        sc_a[red, o] = sc_t[red]

        def finish():
            for k in range(1, ops):
                pltpu.make_async_remote_copy(
                    sc_t.at[red], sc_a.at[red, op_at[k]], a_send.at[red, k], a_recv.at[red, k],
                    device_id=(z, op_at[k]), device_id_type=MESH).wait_recv()
            sc_b[red, z] = jnp.sum(sc_a[red], axis=0)
            for d in range(1, sectors):
                copy = pltpu.make_async_remote_copy(
                    sc_b.at[red, z], sc_b.at[red, z], b_send.at[red, d], b_recv.at[red, d],
                    device_id=(z_at[d], o), device_id_type=MESH)
                copy.start()
                sent.append(copy)
            for d in range(1, sectors):
                pltpu.make_async_remote_copy(
                    sc_b.at[red, z], sc_b.at[red, z_at[d]], b_send.at[red, d], b_recv.at[red, d],
                    device_id=(z_at[d], o), device_id_type=MESH).wait_recv()
            both = jnp.sum(sc_b[red], axis=0)
            for copy in sent:
                copy.wait_send()
            return both

        return finish

    scale = None
    for step in range(STEPS):
        groups = (xa.at[step], xb.at[step])

        sent = []

        def slot(d, g, other):
            return groups[1 if g >= half else 0].at[d, pl.ds(row_at[g][other], rows), :]

        def send(d, g, to, to_d, to_g, other):
            copy = pltpu.make_async_remote_copy(
                slot(d, g, 0),
                groups[1 if to_g >= half else 0].at[to_d, pl.ds(row_at[g][0], rows), :],
                x_send.at[step, len(sent)], x_recv.at[step, to_d, to_g, other],
                device_id=to, device_id_type=MESH)
            copy.start()
            sent.append(copy)

        def arrive(d, g, other):
            here = slot(d, g, other)
            pltpu.make_async_remote_copy(
                here, here, x_send.at[step, 0], x_recv.at[step, d, g, other],
                device_id=(z, op_at[1]), device_id_type=MESH).wait_recv()

        groups[0][0, pl.ds(row_at[0][0], rows), :] = cur[...].astype(BF16)

        def spread(d, g):
            if d or g:
                arrive(d, g, 0)
            order = list(range(bits)) if d % 2 == 0 else list(range(bits))[::-1]
            last = -1
            for at, bit in enumerate(order):
                if g & (1 << bit):
                    last = at
            if d == 0 and g == 0 and sectors > 1:
                send(0, 0, (z_at[1], o), 1, 0, 0)
            for bit in order[last + 1 :]:
                send(d, g, (z, op_at[2 << bit]), d, g ^ (1 << bit), 0)
            if d == 0 and g == 0:
                for far in range(2, sectors):
                    send(0, 0, (z_at[far], o), far, 0, 0)
            send(d, g, (z, op_at[1]), d, g, 1)

        level = lambda g: bin(g).count("1")
        is_late = lambda dg: dg[1] >= half and level(dg[1]) > 1
        plan = [(d, g) for d in range(sectors) for g in range(chips)]
        plan.sort(key=lambda dg: (is_late(dg), dg[0] + level(dg[1]), dg))
        early = [dg for dg in plan if not is_late(dg)]
        late = [dg for dg in plan if is_late(dg)]

        def rotate(which):
            for p in range(pairs):
                x = groups[which][coup[z, o * pairs + p] ^ z]
                t = lax.dot_general(x, rv[p], (((1,), (1,)), ((), ())), preferred_element_type=F32)
                tt[p, pl.ds(first_at[which], half_rows), :] = t.astype(BF16)

        def arrive_sibling(first, end):
            for d in range(sectors):
                for g in range(first, end):
                    arrive(d, g, 1)

        for d, g in early:
            spread(d, g)
        arrive_sibling(0, half)
        if step == 0:
            small[2].wait()
            loads[0].wait()
        rotate(0)
        for d, g in late:
            spread(d, g)
        arrive_sibling(half, chips)
        rotate(1)
        if step == 0:
            for load in loads[1:] + small[3:]:
                load.wait()

        def r1(g):
            return pltpu.make_async_remote_copy(
                s1_tx.at[step, g], s1_rx.at[step, g], r1_send.at[step, g], r1_recv.at[step, g],
                device_id=(z, op_at[1]), device_id_type=MESH)

        def r2(g):
            return pltpu.make_async_remote_copy(
                s2_tx.at[step, g], s2_rx.at[step, g], r2_send.at[step, g], r2_recv.at[step, g],
                device_id=(z, op_at[2 * g]), device_id_type=MESH)

        def block(g, other):
            return acc[1 if g >= half else 0, pl.ds(row_at[g][other], rows), :]

        def partial(which, first, end):
            total = None
            for p in range(first, end):
                part = jnp.dot(
                    lv[p, pl.ds(first_at[which], half_rows), :], tt[p], preferred_element_type=F32)
                total = part if total is None else total + part
            return total

        def to_sibling(which):
            for g in reversed(range(which * half, which * half + half)):
                s1_tx[step, g] = block(g, 1).astype(BF16)
                r1(g).start()

        def to_chips(which):
            for g in reversed(range(max(1, which * half), which * half + half)):
                r1(g).wait_recv()
                s2_tx[step, g] = (block(g, 0) + s1_rx[step, g].astype(F32)).astype(BF16)
                r2(g).start()

        acc[1] = partial(1, 0, pairs)
        to_sibling(1)
        acc[0] = partial(0, 0, pairs // 2)
        to_chips(1)
        acc[0] += partial(0, pairs // 2, pairs)
        to_sibling(0)
        sc_t[step, 0] = (
            folded(xa[step, 0].astype(F32) * acc[0]) + folded(xb[step, 0].astype(F32) * acc[1])
        )
        sc_t[step, 1] = folded(cur[...] * cur[...])
        finish = reduce_tile(step)
        to_chips(0)
        both = finish()
        r1(0).wait_recv()
        sigma = block(0, 0) + s1_rx[step, 0].astype(F32)
        for g in range(1, chips):
            r2(g).wait_recv()
            sigma = sigma + s2_rx[step, g].astype(F32)
        sigma = sigma * mask
        numer, denom = total_of(both[0]), total_of(both[1])
        if step == 0:
            theta = numer / (denom + 1e-06)
        else:
            scale = lax.rsqrt(denom / entry_total + 1e-06)
            theta = (scale * scale * numer) / (scale * scale * denom + 1e-06)
        energies[step] = theta[0, 0]
        gap = diag[...] - theta
        held = cur[...]
        update = held - (sigma - theta * held) * (gap / (gap * gap + 1.0))
        if step > 0:
            update = update * scale
        cur[...] = update
        for copy in sent:
            copy.wait_send()
        for g in range(chips):
            r1(g).wait_send()
        for g in range(1, chips):
            r2(g).wait_send()

    sc_t[STEPS, 0] = folded(cur[...] * cur[...])
    sc_t[STEPS, 1] = jnp.zeros((8, 128), F32)
    squares = total_of(reduce_tile(STEPS)()[0])
    vec[...] = cur[...] * lax.rsqrt(squares / entry_total + 1e-06)


def shards(sectors, ops, wavefunction, diagonal, left_blocks, right_blocks, coupling, sector_sizes):
    _, rows, width = wavefunction.shape
    pairs = left_blocks.shape[0]
    chips = ops // 2
    half_rows = ops * rows // 2
    entry_total = float(wavefunction.size * sectors * ops)
    vmem = pl.BlockSpec(memory_space=pltpu.VMEM)
    smem = pl.BlockSpec(memory_space=pltpu.SMEM)
    hbm = pl.BlockSpec(memory_space=pl.ANY)
    dma = pltpu.SemaphoreType.DMA
    vector, energies = pl.pallas_call(
        functools.partial(kernel, sectors, ops, entry_total),
        out_shape=(
            jax.ShapeDtypeStruct((rows, width), F32),
            jax.ShapeDtypeStruct((STEPS,), F32),
        ),
        in_specs=[hbm] * 6,
        out_specs=(vmem, smem),
        scratch_shapes=[
            pltpu.SMEM(coupling.shape, jnp.int32),
            pltpu.SMEM(sector_sizes.shape, jnp.int32),
            pltpu.VMEM((rows, width), F32),
            pltpu.VMEM((rows, width), F32),
            pltpu.VMEM(left_blocks.shape, BF16),
            pltpu.VMEM(right_blocks.shape, BF16),
            pltpu.VMEM((STEPS, sectors, half_rows, width), BF16),
            pltpu.VMEM((STEPS, sectors, half_rows, width), BF16),
            pltpu.VMEM(left_blocks.shape, BF16),
            pltpu.VMEM((2, half_rows, width), F32),
            pltpu.VMEM((rows, width), F32),
            pltpu.VMEM((STEPS, chips, rows, width), BF16),
            pltpu.VMEM((STEPS, chips, rows, width), BF16),
            pltpu.VMEM((STEPS, chips, rows, width), BF16),
            pltpu.VMEM((STEPS, chips, rows, width), BF16),
            pltpu.VMEM((STEPS + 1, ops, 2, 8, 128), F32),
            pltpu.VMEM((STEPS + 1, sectors, 2, 8, 128), F32),
            pltpu.VMEM((STEPS + 1, 2, 8, 128), F32),
            dma((6,)),
            dma((STEPS, sectors * ops)),
            dma((STEPS, sectors, chips, 2)),
            dma((STEPS, chips)),
            dma((STEPS, chips)),
            dma((STEPS, chips)),
            dma((STEPS, chips)),
            dma((STEPS + 1, ops)),
            dma((STEPS + 1, ops)),
            dma((STEPS + 1, sectors)),
            dma((STEPS + 1, sectors)),
        ],
        compiler_params=pltpu.CompilerParams(
            collective_id=0, has_side_effects=True, vmem_limit_bytes=62 * 1024 * 1024
        ),
    )(coupling, sector_sizes, wavefunction[0], diagonal[0], left_blocks, right_blocks)
    return vector[None], energies


def solution(mesh):
    in_specs = (
        P("sector", "op", None),
        P("sector", "op", None),
        P("op", None, None),
        P("op", None, None),
        P(),
        P(),
    )
    out_specs = (P("sector", "op", None), P())
    body = functools.partial(shards, mesh.shape["sector"], mesh.shape["op"])
    return jax.shard_map(body, mesh=mesh, in_specs=in_specs, out_specs=out_specs, check_vma=False)
```

```python
import functools

import jax
import jax.numpy as jnp
from jax import lax
from jax.experimental import pallas as pl
from jax.experimental.pallas import tpu as pltpu
from jax.sharding import PartitionSpec as P

STEPS = 2
MESH = pl.DeviceIdType.MESH
F32 = jnp.float32
BF16 = jnp.bfloat16


def flip(value, mask):
    bit = 1
    while bit <= mask:
        if mask & bit:
            value = value + bit - 2 * bit * ((value // bit) % 2)
        bit *= 2
    return value


def folded(x):
    rows, width = x.shape
    x = jnp.sum(x.reshape(rows // 8, 8, width), axis=0)
    total = x[:, 0:128]
    for at in range(128, width, 128):
        total = total + x[:, at : at + 128]
    return total


def total_of(tile):
    return jnp.sum(jnp.sum(tile, axis=0, keepdims=True), axis=1, keepdims=True)


def kernel(
    sectors, ops, entry_total,
    coup_in, sizes_in, wf_in, diag_in, left, right,
    vec, energies,
    coup, sizes, wf, diag, lv, rv, xa, xb, tt, acc, cur, s1_tx, s1_rx, s2_tx, s2_rx, sc_a, sc_b, sc_t,
    load_sem, x_send, x_recv, r1_send, r1_recv, r2_send, r2_recv, a_send, a_recv, b_send, b_recv,
):
    rows, width = wf.shape
    pairs = left.shape[0]
    chips = ops // 2
    half = chips // 2
    bits = chips.bit_length() - 1
    half_rows = half * 2 * rows
    z = lax.axis_index("sector")
    o = lax.axis_index("op")
    m, c = o // 2, o % 2
    top = m // half
    chip_at = [flip(m, g) for g in range(chips)]
    op_at = [flip(o, k) for k in range(ops)]
    z_at = [flip(z, d) for d in range(sectors)]
    row_at = [
        [pl.multiple_of((chip_at[g] % half) * (2 * rows) + core * rows, rows) for core in (c, 1 - c)]
        for g in range(chips)
    ]
    first_at = [pl.multiple_of(at * half_rows, half_rows) for at in (top, 1 - top)]

    small = [(wf_in, wf), (sizes_in, sizes), (coup_in, coup), (diag_in, diag)]
    small = [
        pltpu.make_async_copy(src, dst, load_sem.at[at]) for at, (src, dst) in enumerate(small)
    ]
    loads = [
        pltpu.make_async_copy(right, rv, load_sem.at[4]),
        pltpu.make_async_copy(left, lv, load_sem.at[5]),
    ]
    for load in small:
        load.start()

    barrier = pltpu.get_barrier_semaphore()
    for k in range(1, ops):
        pl.semaphore_signal(barrier, inc=1, device_id=(z, op_at[k]), device_id_type=MESH)
    for d in range(1, sectors):
        pl.semaphore_signal(barrier, inc=1, device_id=(z_at[d], o), device_id_type=MESH)

    small[0].wait()
    small[1].wait()
    bound = sizes[z]
    row_ids = o * rows + lax.broadcasted_iota(jnp.int32, (rows, width), 0)
    col_ids = lax.broadcasted_iota(jnp.int32, (rows, width), 1)
    mask = ((row_ids < bound) & (col_ids < bound)).astype(F32)
    cur[...] = wf[...] * mask
    pl.semaphore_wait(barrier, ops - 1 + sectors - 1)

    def reduce_tile(red):
        sent = []
        for k in range(1, ops):
            copy = pltpu.make_async_remote_copy(
                sc_t.at[red], sc_a.at[red, o], a_send.at[red, k], a_recv.at[red, k],
                device_id=(z, op_at[k]), device_id_type=MESH)
            copy.start()
            sent.append(copy)
        sc_a[red, o] = sc_t[red]

        def finish():
            for k in range(1, ops):
                pltpu.make_async_remote_copy(
                    sc_t.at[red], sc_a.at[red, op_at[k]], a_send.at[red, k], a_recv.at[red, k],
                    device_id=(z, op_at[k]), device_id_type=MESH).wait_recv()
            sc_b[red, z] = jnp.sum(sc_a[red], axis=0)
            for d in range(1, sectors):
                copy = pltpu.make_async_remote_copy(
                    sc_b.at[red, z], sc_b.at[red, z], b_send.at[red, d], b_recv.at[red, d],
                    device_id=(z_at[d], o), device_id_type=MESH)
                copy.start()
                sent.append(copy)
            for d in range(1, sectors):
                pltpu.make_async_remote_copy(
                    sc_b.at[red, z], sc_b.at[red, z_at[d]], b_send.at[red, d], b_recv.at[red, d],
                    device_id=(z_at[d], o), device_id_type=MESH).wait_recv()
            both = jnp.sum(sc_b[red], axis=0)
            for copy in sent:
                copy.wait_send()
            return both

        return finish

    scale = None
    for step in range(STEPS):
        groups = (xa.at[step], xb.at[step])

        sent = []

        def slot(d, g, other):
            return groups[1 if g >= half else 0].at[d, pl.ds(row_at[g][other], rows), :]

        def send(d, g, to, to_d, to_g, other):
            copy = pltpu.make_async_remote_copy(
                slot(d, g, 0),
                groups[1 if to_g >= half else 0].at[to_d, pl.ds(row_at[g][0], rows), :],
                x_send.at[step, len(sent)], x_recv.at[step, to_d, to_g, other],
                device_id=to, device_id_type=MESH)
            copy.start()
            sent.append(copy)

        def arrive(d, g, other):
            here = slot(d, g, other)
            pltpu.make_async_remote_copy(
                here, here, x_send.at[step, 0], x_recv.at[step, d, g, other],
                device_id=(z, op_at[1]), device_id_type=MESH).wait_recv()

        groups[0][0, pl.ds(row_at[0][0], rows), :] = cur[...].astype(BF16)

        def spread(d, g):
            if d or g:
                arrive(d, g, 0)
            order = list(range(bits)) if d < sectors // 2 else list(range(bits))[::-1]
            last = -1
            for at, bit in enumerate(order):
                if g & (1 << bit):
                    last = at
            if d == 0 and g == 0:
                for far in range(1, sectors):
                    send(0, 0, (z_at[far], o), far, 0, 0)
            for bit in order[last + 1 :]:
                send(d, g, (z, op_at[2 << bit]), d, g ^ (1 << bit), 0)
            send(d, g, (z, op_at[1]), d, g, 1)
            if step == 0 and d == 0 and g == 0:
                for load in loads:
                    load.start()

        level = lambda g: bin(g).count("1")
        is_late = lambda dg: dg[1] >= half and level(dg[1]) > 1
        plan = [(d, g) for d in range(sectors) for g in range(chips)]
        plan.sort(key=lambda dg: (is_late(dg), dg[0] + level(dg[1]), level(dg[1]), dg))
        early = [dg for dg in plan if not is_late(dg)]
        late = [dg for dg in plan if is_late(dg)]

        def rotate(which):
            for p in range(pairs):
                x = groups[which][coup[z, o * pairs + p] ^ z]
                t = lax.dot_general(x, rv[p], (((1,), (1,)), ((), ())), preferred_element_type=F32)
                tt[p, pl.ds(first_at[which], half_rows), :] = t.astype(BF16)

        def arrive_sibling(first, end):
            for d in range(sectors):
                for g in range(first, end):
                    arrive(d, g, 1)

        for d, g in early:
            spread(d, g)
        arrive_sibling(0, half)
        if step == 0:
            small[2].wait()
            loads[0].wait()
        rotate(0)
        for d, g in late:
            spread(d, g)
        arrive_sibling(half, chips)
        rotate(1)
        if step == 0:
            for load in loads[1:] + small[3:]:
                load.wait()

        def r1(g):
            return pltpu.make_async_remote_copy(
                s1_tx.at[step, g], s1_rx.at[step, g], r1_send.at[step, g], r1_recv.at[step, g],
                device_id=(z, op_at[1]), device_id_type=MESH)

        def r2(g):
            return pltpu.make_async_remote_copy(
                s2_tx.at[step, g], s2_rx.at[step, g], r2_send.at[step, g], r2_recv.at[step, g],
                device_id=(z, op_at[2 * g]), device_id_type=MESH)

        def block(g, other):
            return acc[1 if g >= half else 0, pl.ds(row_at[g][other], rows), :]

        def partial(which, first, end):
            total = None
            for p in range(first, end):
                part = jnp.dot(
                    lv[p, pl.ds(first_at[which], half_rows), :], tt[p], preferred_element_type=F32)
                total = part if total is None else total + part
            return total

        def to_sibling(which):
            for g in reversed(range(which * half, which * half + half)):
                s1_tx[step, g] = block(g, 1).astype(BF16)
                r1(g).start()

        def to_chips(which):
            for g in reversed(range(max(1, which * half), which * half + half)):
                r1(g).wait_recv()
                s2_tx[step, g] = (block(g, 0) + s1_rx[step, g].astype(F32)).astype(BF16)
                r2(g).start()

        acc[1] = partial(1, 0, pairs)
        to_sibling(1)
        acc[0] = partial(0, 0, pairs)
        to_sibling(0)
        sc_t[step, 0] = (
            folded(xa[step, 0].astype(F32) * acc[0]) + folded(xb[step, 0].astype(F32) * acc[1])
        )
        sc_t[step, 1] = folded(cur[...] * cur[...])
        finish = reduce_tile(step)
        to_chips(1)
        to_chips(0)
        both = finish()
        r1(0).wait_recv()
        sigma = block(0, 0) + s1_rx[step, 0].astype(F32)
        for g in range(1, chips):
            r2(g).wait_recv()
            sigma = sigma + s2_rx[step, g].astype(F32)
        sigma = sigma * mask
        numer, denom = total_of(both[0]), total_of(both[1])
        if step == 0:
            theta = numer / (denom + 1e-06)
        else:
            scale = lax.rsqrt(denom / entry_total + 1e-06)
            theta = (scale * scale * numer) / (scale * scale * denom + 1e-06)
        energies[step] = theta[0, 0]
        gap = diag[...] - theta
        held = cur[...]
        update = held - (sigma - theta * held) * (gap / (gap * gap + 1.0))
        if step > 0:
            update = update * scale
        cur[...] = update
        for copy in sent:
            copy.wait_send()
        for g in range(chips):
            r1(g).wait_send()
        for g in range(1, chips):
            r2(g).wait_send()

    sc_t[STEPS, 0] = folded(cur[...] * cur[...])
    sc_t[STEPS, 1] = jnp.zeros((8, 128), F32)
    squares = total_of(reduce_tile(STEPS)()[0])
    vec[...] = cur[...] * lax.rsqrt(squares / entry_total + 1e-06)


def shards(sectors, ops, wavefunction, diagonal, left_blocks, right_blocks, coupling, sector_sizes):
    _, rows, width = wavefunction.shape
    pairs = left_blocks.shape[0]
    chips = ops // 2
    half_rows = ops * rows // 2
    entry_total = float(wavefunction.size * sectors * ops)
    vmem = pl.BlockSpec(memory_space=pltpu.VMEM)
    smem = pl.BlockSpec(memory_space=pltpu.SMEM)
    hbm = pl.BlockSpec(memory_space=pl.ANY)
    dma = pltpu.SemaphoreType.DMA
    vector, energies = pl.pallas_call(
        functools.partial(kernel, sectors, ops, entry_total),
        out_shape=(
            jax.ShapeDtypeStruct((rows, width), F32),
            jax.ShapeDtypeStruct((STEPS,), F32),
        ),
        in_specs=[hbm] * 6,
        out_specs=(vmem, smem),
        scratch_shapes=[
            pltpu.SMEM(coupling.shape, jnp.int32),
            pltpu.SMEM(sector_sizes.shape, jnp.int32),
            pltpu.VMEM((rows, width), F32),
            pltpu.VMEM((rows, width), F32),
            pltpu.VMEM(left_blocks.shape, BF16),
            pltpu.VMEM(right_blocks.shape, BF16),
            pltpu.VMEM((STEPS, sectors, half_rows, width), BF16),
            pltpu.VMEM((STEPS, sectors, half_rows, width), BF16),
            pltpu.VMEM(left_blocks.shape, BF16),
            pltpu.VMEM((2, half_rows, width), F32),
            pltpu.VMEM((rows, width), F32),
            pltpu.VMEM((STEPS, chips, rows, width), BF16),
            pltpu.VMEM((STEPS, chips, rows, width), BF16),
            pltpu.VMEM((STEPS, chips, rows, width), BF16),
            pltpu.VMEM((STEPS, chips, rows, width), BF16),
            pltpu.VMEM((STEPS + 1, ops, 2, 8, 128), F32),
            pltpu.VMEM((STEPS + 1, sectors, 2, 8, 128), F32),
            pltpu.VMEM((STEPS + 1, 2, 8, 128), F32),
            dma((6,)),
            dma((STEPS, sectors * ops)),
            dma((STEPS, sectors, chips, 2)),
            dma((STEPS, chips)),
            dma((STEPS, chips)),
            dma((STEPS, chips)),
            dma((STEPS, chips)),
            dma((STEPS + 1, ops)),
            dma((STEPS + 1, ops)),
            dma((STEPS + 1, sectors)),
            dma((STEPS + 1, sectors)),
        ],
        compiler_params=pltpu.CompilerParams(
            collective_id=0, has_side_effects=True, vmem_limit_bytes=62 * 1024 * 1024
        ),
    )(coupling, sector_sizes, wavefunction[0], diagonal[0], left_blocks, right_blocks)
    return vector[None], energies


def solution(mesh):
    in_specs = (
        P("sector", "op", None),
        P("sector", "op", None),
        P("op", None, None),
        P("op", None, None),
        P(),
        P(),
    )
    out_specs = (P("sector", "op", None), P())
    body = functools.partial(shards, mesh.shape["sector"], mesh.shape["op"])
    return jax.shard_map(body, mesh=mesh, in_specs=in_specs, out_specs=out_specs, check_vma=False)
```

```python
import functools

import jax
import jax.numpy as jnp
from jax import lax
from jax.experimental import pallas as pl
from jax.experimental.pallas import tpu as pltpu
from jax.sharding import PartitionSpec as P

STEPS = 2
MESH = pl.DeviceIdType.MESH
F32 = jnp.float32
BF16 = jnp.bfloat16


def flip(value, mask):
    bit = 1
    while bit <= mask:
        if mask & bit:
            value = value + bit - 2 * bit * ((value // bit) % 2)
        bit *= 2
    return value


def folded(x):
    rows, width = x.shape
    x = jnp.sum(x.reshape(rows // 8, 8, width), axis=0)
    total = x[:, 0:128]
    for at in range(128, width, 128):
        total = total + x[:, at : at + 128]
    return total


def total_of(tile):
    return jnp.sum(jnp.sum(tile, axis=0, keepdims=True), axis=1, keepdims=True)


def kernel(
    sectors, ops, entry_total,
    coup_in, sizes_in, wf_in, diag_in, left, right,
    vec, energies,
    coup, sizes, wf, diag, lv, rv, xa, xb, tt, acc, cur, s1_tx, s1_rx, s2_tx, s2_rx, sc_a, sc_b, sc_t,
    load_sem, x_send, x_recv, r1_send, r1_recv, r2_send, r2_recv, a_send, a_recv, b_send, b_recv,
):
    rows, width = wf.shape
    pairs = left.shape[0]
    chips = ops // 2
    half = chips // 2
    bits = chips.bit_length() - 1
    half_rows = half * 2 * rows
    z = lax.axis_index("sector")
    o = lax.axis_index("op")
    m, c = o // 2, o % 2
    top = m // half
    chip_at = [flip(m, g) for g in range(chips)]
    op_at = [flip(o, k) for k in range(ops)]
    z_at = [flip(z, d) for d in range(sectors)]
    row_at = [
        [pl.multiple_of((chip_at[g] % half) * (2 * rows) + core * rows, rows) for core in (c, 1 - c)]
        for g in range(chips)
    ]
    first_at = [pl.multiple_of(at * half_rows, half_rows) for at in (top, 1 - top)]
    valid = {r: jnp.logical_and(z + r >= 0, z + r < sectors) for r in range(1 - sectors, sectors)}

    small = [(wf_in, wf), (sizes_in, sizes), (coup_in, coup), (diag_in, diag)]
    small = [
        pltpu.make_async_copy(src, dst, load_sem.at[at]) for at, (src, dst) in enumerate(small)
    ]
    loads = [
        pltpu.make_async_copy(right, rv, load_sem.at[4]),
        pltpu.make_async_copy(left, lv, load_sem.at[5]),
    ]
    for load in small:
        load.start()

    barrier = pltpu.get_barrier_semaphore()
    for k in range(1, ops):
        pl.semaphore_signal(barrier, inc=1, device_id=(z, op_at[k]), device_id_type=MESH)
    for d in range(1, sectors):
        pl.semaphore_signal(barrier, inc=1, device_id=(z_at[d], o), device_id_type=MESH)

    small[0].wait()
    small[1].wait()
    bound = sizes[z]
    row_ids = o * rows + lax.broadcasted_iota(jnp.int32, (rows, width), 0)
    col_ids = lax.broadcasted_iota(jnp.int32, (rows, width), 1)
    mask = ((row_ids < bound) & (col_ids < bound)).astype(F32)
    cur[...] = wf[...] * mask
    pl.semaphore_wait(barrier, ops - 1 + sectors - 1)

    def reduce_tile(red):
        sent = []
        for k in range(1, ops):
            copy = pltpu.make_async_remote_copy(
                sc_t.at[red], sc_a.at[red, o], a_send.at[red, k], a_recv.at[red, k],
                device_id=(z, op_at[k]), device_id_type=MESH)
            copy.start()
            sent.append(copy)
        sc_a[red, o] = sc_t[red]

        def finish():
            for k in range(1, ops):
                pltpu.make_async_remote_copy(
                    sc_t.at[red], sc_a.at[red, op_at[k]], a_send.at[red, k], a_recv.at[red, k],
                    device_id=(z, op_at[k]), device_id_type=MESH).wait_recv()
            sc_b[red, z] = jnp.sum(sc_a[red], axis=0)
            for d in range(1, sectors):
                copy = pltpu.make_async_remote_copy(
                    sc_b.at[red, z], sc_b.at[red, z], b_send.at[red, d], b_recv.at[red, d],
                    device_id=(z_at[d], o), device_id_type=MESH)
                copy.start()
                sent.append(copy)
            for d in range(1, sectors):
                pltpu.make_async_remote_copy(
                    sc_b.at[red, z], sc_b.at[red, z_at[d]], b_send.at[red, d], b_recv.at[red, d],
                    device_id=(z_at[d], o), device_id_type=MESH).wait_recv()
            both = jnp.sum(sc_b[red], axis=0)
            for copy in sent:
                copy.wait_send()
            return both

        return finish

    scale = None
    for step in range(STEPS):
        groups = (xa.at[step], xb.at[step])

        def place(r, g, core):
            return z + r, row_at[g][core], op_at[2 * g + core]

        sent = []

        def inside(r):
            return valid[r]

        def send(pred, r, g, to, to_g):
            at = len(sent)

            def copy():
                sector, row, owner = place(r, g, 0)
                source = groups[1 if g >= half else 0].at[sector, pl.ds(row, rows), :]
                target = groups[1 if to_g >= half else 0].at[sector, pl.ds(row, rows), :]
                return pltpu.make_async_remote_copy(
                    source, target, x_send.at[at], x_recv.at[step, sector, owner],
                    device_id=to, device_id_type=MESH)

            sent.append((pred, copy))
            pl.when(pred)(lambda: copy().start())

        def arrive(r, g, core):
            sector, row, owner = place(r, g, core)
            slot = groups[1 if g >= half else 0].at[sector, pl.ds(row, rows), :]
            pltpu.make_async_remote_copy(
                slot, slot, x_send.at[0], x_recv.at[step, sector, owner],
                device_id=(z, op_at[1]), device_id_type=MESH).wait_recv()

        own_sector, own_row, _ = place(0, 0, 0)
        groups[0][own_sector, pl.ds(own_row, rows), :] = cur[...].astype(BF16)

        def spread(r, g):
            here = inside(r)
            if r or g:
                pl.when(here)(lambda: arrive(r, g, 0))
            if g == 0 and r <= 0:
                send(jnp.logical_and(here, z + 1 < sectors), r, 0, (z + 1, o), 0)
            if g == 0 and r >= 0:
                send(jnp.logical_and(here, z >= 1), r, 0, (z - 1, o), 0)
            order = list(range(bits)) if r % 2 == 0 else list(range(bits))[::-1]
            last = -1
            for at, bit in enumerate(order):
                if g & (1 << bit):
                    last = at
            for bit in order[last + 1 :]:
                send(here, r, g, (z, op_at[2 << bit]), g ^ (1 << bit))
            send(here, r, g, (z, op_at[1]), g)
            if step == 0 and r == 0 and g == 0:
                for load in loads:
                    load.start()

        def arrive_sibling(first, end):
            for r in range(1 - sectors, sectors):

                @pl.when(inside(r))
                def _():
                    for g in range(first, end):
                        arrive(r, g, 1)

        level = lambda g: bin(g).count("1")
        is_late = lambda rg: rg[1] >= half and level(rg[1]) > 1
        plan = [(r, g) for r in range(1 - sectors, sectors) for g in range(chips)]
        plan.sort(key=lambda rg: (is_late(rg), abs(rg[0]) + level(rg[1]), level(rg[1]), abs(rg[0]), rg))
        early = [rg for rg in plan if not is_late(rg)]
        late = [rg for rg in plan if is_late(rg)]

        def rotate(group, at):
            first = pl.multiple_of(at * half_rows, half_rows)
            for p in range(pairs):
                x = group[coup[z, o * pairs + p]]
                t = lax.dot_general(x, rv[p], (((1,), (1,)), ((), ())), preferred_element_type=F32)
                tt[p, pl.ds(first, half_rows), :] = t.astype(BF16)

        for r, g in early:
            spread(r, g)
        arrive_sibling(0, half)
        if step == 0:
            small[2].wait()
            loads[0].wait()
        rotate(groups[0], top)
        for r, g in late:
            spread(r, g)
        arrive_sibling(half, chips)
        rotate(groups[1], 1 - top)
        if step == 0:
            for load in loads[1:] + small[3:]:
                load.wait()

        def r1(g):
            return pltpu.make_async_remote_copy(
                s1_tx.at[step, g], s1_rx.at[step, g], r1_send.at[step, g], r1_recv.at[step, g],
                device_id=(z, op_at[1]), device_id_type=MESH)

        def r2(g):
            return pltpu.make_async_remote_copy(
                s2_tx.at[step, g], s2_rx.at[step, g], r2_send.at[step, g], r2_recv.at[step, g],
                device_id=(z, op_at[2 * g]), device_id_type=MESH)

        def block(which, g, core):
            return acc[which, pl.ds(row_at[g][core], rows), :]

        def partial(which):
            total = None
            for p in range(pairs):
                part = jnp.dot(
                    lv[p, pl.ds(first_at[which], half_rows), :], tt[p], preferred_element_type=F32)
                total = part if total is None else total + part
            acc[which] = total

        def to_sibling(which):
            for g in reversed(range(which * half, which * half + half)):
                s1_tx[step, g] = block(which, g, 1).astype(BF16)
                r1(g).start()

        def to_chips(which):
            for g in reversed(range(max(1, which * half), which * half + half)):
                r1(g).wait_recv()
                s2_tx[step, g] = (block(which, g, 0) + s1_rx[step, g].astype(F32)).astype(BF16)
                r2(g).start()

        partial(1)
        to_sibling(1)
        partial(0)
        to_sibling(0)
        sc_t[step, 0] = folded(xa[step, z].astype(F32) * acc[0]) + folded(xb[step, z].astype(F32) * acc[1])
        sc_t[step, 1] = folded(cur[...] * cur[...])
        finish = reduce_tile(step)
        to_chips(1)
        to_chips(0)
        both = finish()
        r1(0).wait_recv()
        sigma = block(0, 0, 0) + s1_rx[step, 0].astype(F32)
        for g in range(1, chips):
            r2(g).wait_recv()
            sigma = sigma + s2_rx[step, g].astype(F32)
        sigma = sigma * mask
        numer, denom = total_of(both[0]), total_of(both[1])
        if step == 0:
            theta = numer / (denom + 1e-06)
        else:
            scale = lax.rsqrt(denom / entry_total + 1e-06)
            theta = (scale * scale * numer) / (scale * scale * denom + 1e-06)
        energies[step] = theta[0, 0]
        gap = diag[...] - theta
        held = cur[...]
        update = held - (sigma - theta * held) * (gap / (gap * gap + 1.0))
        if step > 0:
            update = update * scale
        cur[...] = update
        for pred, copy in sent:
            pl.when(pred)(lambda copy=copy: copy().wait_send())
        for g in range(chips):
            r1(g).wait_send()
        for g in range(1, chips):
            r2(g).wait_send()

    sc_t[STEPS, 0] = folded(cur[...] * cur[...])
    sc_t[STEPS, 1] = jnp.zeros((8, 128), F32)
    squares = total_of(reduce_tile(STEPS)()[0])
    vec[...] = cur[...] * lax.rsqrt(squares / entry_total + 1e-06)


def shards(sectors, ops, wavefunction, diagonal, left_blocks, right_blocks, coupling, sector_sizes):
    _, rows, width = wavefunction.shape
    pairs = left_blocks.shape[0]
    chips = ops // 2
    half_rows = ops * rows // 2
    entry_total = float(wavefunction.size * sectors * ops)
    vmem = pl.BlockSpec(memory_space=pltpu.VMEM)
    smem = pl.BlockSpec(memory_space=pltpu.SMEM)
    hbm = pl.BlockSpec(memory_space=pl.ANY)
    dma = pltpu.SemaphoreType.DMA
    sends = (2 * sectors - 1) * 2 * chips + 2
    vector, energies = pl.pallas_call(
        functools.partial(kernel, sectors, ops, entry_total),
        out_shape=(
            jax.ShapeDtypeStruct((rows, width), F32),
            jax.ShapeDtypeStruct((STEPS,), F32),
        ),
        in_specs=[hbm] * 6,
        out_specs=(vmem, smem),
        scratch_shapes=[
            pltpu.SMEM(coupling.shape, jnp.int32),
            pltpu.SMEM(sector_sizes.shape, jnp.int32),
            pltpu.VMEM((rows, width), F32),
            pltpu.VMEM((rows, width), F32),
            pltpu.VMEM(left_blocks.shape, BF16),
            pltpu.VMEM(right_blocks.shape, BF16),
            pltpu.VMEM((STEPS, sectors, half_rows, width), BF16),
            pltpu.VMEM((STEPS, sectors, half_rows, width), BF16),
            pltpu.VMEM(left_blocks.shape, BF16),
            pltpu.VMEM((2, half_rows, width), F32),
            pltpu.VMEM((rows, width), F32),
            pltpu.VMEM((STEPS, chips, rows, width), BF16),
            pltpu.VMEM((STEPS, chips, rows, width), BF16),
            pltpu.VMEM((STEPS, chips, rows, width), BF16),
            pltpu.VMEM((STEPS, chips, rows, width), BF16),
            pltpu.VMEM((STEPS + 1, ops, 2, 8, 128), F32),
            pltpu.VMEM((STEPS + 1, sectors, 2, 8, 128), F32),
            pltpu.VMEM((STEPS + 1, 2, 8, 128), F32),
            dma((6,)),
            dma((sends,)),
            dma((STEPS, sectors, ops)),
            dma((STEPS, chips)),
            dma((STEPS, chips)),
            dma((STEPS, chips)),
            dma((STEPS, chips)),
            dma((STEPS + 1, ops)),
            dma((STEPS + 1, ops)),
            dma((STEPS + 1, sectors)),
            dma((STEPS + 1, sectors)),
        ],
        compiler_params=pltpu.CompilerParams(
            collective_id=0, has_side_effects=True, vmem_limit_bytes=62 * 1024 * 1024
        ),
    )(coupling, sector_sizes, wavefunction[0], diagonal[0], left_blocks, right_blocks)
    return vector[None], energies


def solution(mesh):
    in_specs = (
        P("sector", "op", None),
        P("sector", "op", None),
        P("op", None, None),
        P("op", None, None),
        P(),
        P(),
    )
    out_specs = (P("sector", "op", None), P())
    body = functools.partial(shards, mesh.shape["sector"], mesh.shape["op"])
    return jax.shard_map(body, mesh=mesh, in_specs=in_specs, out_specs=out_specs, check_vma=False)
```
